512 devices in a mesh: row: 8 (over y, z_hi), col: 16 (over z_lo, core), rep: 4 (over x).
Axes of the slice: x: 4, y: 4, z: 16 (z_hi: 2, z_lo: 8; z = z_hi * 8 + z_lo), core: 2. Of those that a mesh axis runs over, the one named last changes fastest.
Arguments:
- amplitudes: float32 [18432, 18432], P('row', ('col', 'rep')), may hold values from -0.046875 to 0.046875
- cycle_ints: float32 [18432, 1152], P(('col', 'rep'), 'row'), may hold values from -16 to 16
Outputs:
- cycle_term: float32 [18432, 1152], P(('row', 'rep'), 'col')
The draws below stay inside these ranges and needn't reach their ends.
All inputs are finite; a program needn't handle non-finite values.
Results may differ from the reference program's by a relative error of at most 0.0002.
Values sent between devices are 32-bit elements; how exact they have to be, the bound alone decides.
A program may use at most 64 MiB of HBM per device.

```python
import jax
import jax.numpy as jnp
from jax import lax

PAIRS = 18432
WINDOW = 1152


def raised(drawn, stream_key, source, target, shards_of, factor):
    def block_of(position):
        return (jnp.arange(drawn.shape[position]) // (drawn.shape[position] // shards_of)).reshape((-1,) + (1,) * (drawn.ndim - 1 - position))

    near = jax.random.permutation(stream_key, shards_of)[block_of(target)]
    far = (block_of(target) + shards_of // 2) % shards_of
    return jnp.where((block_of(source) == near) | (block_of(source) == far), factor * drawn, drawn)


def level_of(stream_key, dims, pieces, low, top_value):
    def one(axis_at, shards_of):
        draws = jax.random.uniform(jax.random.fold_in(jax.random.fold_in(stream_key, 6), axis_at), (shards_of,), jnp.float32, low / len(pieces), top_value / len(pieces))
        return jnp.repeat(jnp.exp(draws), dims[axis_at] // shards_of).reshape((-1,) + (1,) * (len(dims) - axis_at - 1))

    gain = one(*pieces[0])
    for cut in pieces[1:]:
        gain = gain * one(*cut)
    return gain


def centred(own_key, shape, scale, bound, pieces=(), kind=jnp.bfloat16):
    array = scale * jax.random.normal(own_key, shape, jnp.float32)
    if pieces:
        array = array * level_of(own_key, shape, pieces, -0.22, 0.18)
    return jnp.clip(array, -bound, bound).astype(kind)


def gaussian_with(own_key, dims, width, limit, pieces, heavy, held_as=jnp.bfloat16):
    drawn = width * jax.random.normal(own_key, dims, jnp.float32)
    if pieces:
        drawn = drawn * level_of(own_key, dims, pieces, -0.22, 0.18)
    return jnp.clip(raised(drawn, jax.random.fold_in(own_key, 3), *heavy), -limit, limit).astype(held_as)


def setup_inputs(seed: int = 0) -> dict:
    splits = jax.random.split(jax.random.key(seed), 3)
    amplitudes = centred(splits[0], (PAIRS, PAIRS), PAIRS ** -0.5, 0.046875, ((0, 8), (1, 64)), jnp.float32)
    cycle_ints = gaussian_with(splits[1], (PAIRS, WINDOW), 1.0, 16.0, ((0, 64), (1, 8)), (0, 1, 64, 4.0), jnp.float32)
    return dict(amplitudes=amplitudes, cycle_ints=cycle_ints)


def reference(amplitudes, cycle_ints):
    return jnp.dot(amplitudes, cycle_ints, precision=lax.Precision.HIGHEST, preferred_element_type=jnp.float32)
```

```python
import functools

import jax
import jax.numpy as jnp
from jax import lax
from jax.experimental import pallas as pl
from jax.experimental.pallas import tpu as pltpu
from jax.sharding import PartitionSpec as P

MESH = pl.DeviceIdType.MESH
STEPS = 8
NX = 4
TOP = 160
UNIT = 328
BOT = UNIT - TOP
LAG = 2


def split(value):
    high = value.astype(jnp.bfloat16)
    return high, (value - high.astype(jnp.float32)).astype(jnp.bfloat16)


def kernel(
    at_ref, bt_ref, out_ref,
    a_own, a_oth, ah, al, b_own, b_oth, bq, pu, opp_l, opp_r, in_l, in_r, z_l, z_r,
    loc_sem, core_s, core_r, b_s, b_r, x_s, x_r, z_s, z_rs,
):
    row, col, x = lax.axis_index("row"), lax.axis_index("col"), lax.axis_index("rep")
    y, h = row // 2, row % 2
    z, c = col // 2, col % 2
    other = {"col": col + 1 - 2 * c}
    right, left, opp = (x + 1) % NX, (x + 3) % NX, (x + 2) % NX
    to_right, to_left = {"rep": right}, {"rep": left}
    twin_row = row + 1 - 2 * h
    y_rows = [(row + 2) % 8, (row + 6) % 8, (row + 4) % 8]

    load_a = [
        pltpu.make_async_copy(
            at_ref.at[:, pl.ds(1152 * p, 1152)], a_own.at[:, pl.ds(1152 * p, 1152)], loc_sem.at[p]
        )
        for p in range(2)
    ]
    load_b = pltpu.make_async_copy(bt_ref, b_own, loc_sem.at[2])
    load_b.start()
    for cp in load_a:
        cp.start()

    barrier = pltpu.get_barrier_semaphore()

    def greet(device):
        pl.semaphore_signal(barrier, inc=1, device_id=device, device_id_type=MESH)

    greet(other)
    greet(to_right)
    greet(to_left)
    for r in y_rows:
        greet({"row": r})
    greet({"row": twin_row})

    @pl.when(z > 0)
    def _():
        greet({"col": col - 2})

    @pl.when(z < 7)
    def _():
        greet({"col": col + 2})

    pl.semaphore_wait(barrier, 7 + jnp.minimum(z, 1) + jnp.minimum(7 - z, 1))

    load_b.wait()
    swap_b = pltpu.make_async_remote_copy(
        b_own.at[pl.ds((1 - c) * 72, 72)], b_oth, core_s.at[0], core_r.at[0],
        device_id=other, device_id_type=MESH,
    )
    swap_b.start()
    swap_a = []
    for p in range(2):
        load_a[p].wait()
        cp = pltpu.make_async_remote_copy(
            a_own.at[:, pl.ds(1152 * p, 1152)], a_oth.at[:, pl.ds(1152 * p, 1152)],
            core_s.at[1 + p], core_r.at[1 + p], device_id=other, device_id_type=MESH,
        )
        cp.start()
        swap_a.append(cp)
    swap_b.wait_recv()
    bq[row, :, 0:576] = jnp.concatenate([b_own[pl.ds(c * 72, 72), :], b_oth[...]], axis=1)

    def send_b(slot, target, sem):
        return pltpu.make_async_remote_copy(
            bq.at[slot], bq.at[slot], b_s.at[sem], b_r.at[slot],
            device_id={"row": target}, device_id_type=MESH,
        )

    sends_b = [send_b(row, twin_row, 0)]
    sends_b += [send_b(row, r, 1 + n) for n, r in enumerate(y_rows)]
    for cp in sends_b:
        cp.start()
    relays_b = [send_b(twin_row, r, 4 + n) for n, r in enumerate(y_rows)]

    def convert(source, base):
        def some(i, _):
            rows = pl.ds(pl.multiple_of(i * 16, 16), 16)
            into = pl.ds(pl.multiple_of(base + i * 16, 16), 16)
            high, low = split(source[rows, :])
            ah[into, :] = high
            al[into, :] = low
            return 0

        lax.fori_loop(0, 18, some, 0, unroll=3)

    convert(a_own, 0)
    for cp in swap_a:
        cp.wait_recv()
    convert(a_oth, 288)

    def order(i):
        near = i + (i // 2) * (1 - 2 * (i % 2))
        first = 2 * ((y + near) % 4) + h
        j = i - 4
        base = (j % 2) * (7 - j) + (1 - j % 2) * j
        last = (1 - h) * 7 + (1 - 2 * (1 - h)) * base
        return jnp.where(i < 4, first, last)

    lanes = lax.broadcasted_iota(jnp.int32, (40, 128), 1)

    def x_copy(kind, i):
        top, bot = pl.ds(0, TOP), pl.ds(TOP, BOT)
        src, dst, device = (
            (pu.at[i, opp, top], opp_l.at[i], to_right),
            (pu.at[i, opp, bot], opp_r.at[i], to_left),
            (pu.at[i, right, bot], in_l.at[i, bot], to_right),
            (pu.at[i, left, top], in_r.at[i, top], to_left),
            (pu.at[i, right, top], in_l.at[i, top], to_right),
            (pu.at[i, left, bot], in_r.at[i, bot], to_left),
        )[kind]
        return pltpu.make_async_remote_copy(
            src, dst, x_s.at[kind, i], x_r.at[kind, i], device_id=device, device_id_type=MESH
        )

    def z_copy(up, i):
        return pltpu.make_async_remote_copy(
            pu.at[i, x], (z_l if up else z_r).at[i],
            z_s.at[0, i], z_rs.at[0 if up else 1, i],
            device_id={"col": col + 2 if up else col - 2}, device_id_type=MESH,
        )

    def product(i):
        d = order(i)

        @pl.when((d != row) & (d != twin_row))
        def _():
            send_b(d, twin_row, 0).wait_recv()

        bh, bl = split(bq[d, :, 0:576])
        for n in range(2):
            p = x // 2 if n else 1 - x // 2
            span = pl.ds(pl.multiple_of(1152 * p, 128), 1152)
            high = ah[:, span]
            v = jnp.dot(bh, high, preferred_element_type=jnp.float32)
            v += jnp.dot(bl, high, preferred_element_type=jnp.float32)
            v += jnp.dot(bh, al[:, span], preferred_element_type=jnp.float32)
            for j in range(4):
                pu[i, 2 * p, 72 * j:72 * j + 72, :] = v[:, 128 * j:128 * j + 128]
                pu[i, 2 * p + 1, 72 * j:72 * j + 72, :] = v[:, 640 + 128 * j:768 + 128 * j]
            up, down = v[0:40, 512:640], v[32:72, 512:640]
            pu[i, 2 * p, 288:328, :] = jnp.where(lanes < 64, up, pltpu.roll(down, 64, 1))
            pu[i, 2 * p + 1, 288:328, :] = jnp.where(lanes < 64, pltpu.roll(up, 64, 1), down)
            if n == 0:
                x_copy(0, i).start()
                x_copy(1, i).start()
        x_copy(2, i).start()
        x_copy(3, i).start()

    def relay(i):
        x_copy(0, i).wait_recv()
        pu[i, right, 0:TOP, :] += opp_l[i]
        x_copy(4, i).start()
        x_copy(1, i).wait_recv()
        pu[i, left, TOP:UNIT, :] += opp_r[i]
        x_copy(5, i).start()

    def gather(i):
        for kind in (2, 4, 3, 5):
            x_copy(kind, i).wait_recv()
        pu[i, x] += in_l[i] + in_r[i]

    def write_out(i):
        v = [pu[i, x, 72 * j:72 * j + 72, :] for j in range(4)]
        tail = pu[i, x, 288:328, :]
        turned = pltpu.roll(tail, 64, 1)
        tail = jnp.concatenate([tail, turned[8:40]], axis=0)

        @pl.when(x % 2 == 0)
        def _():
            for j in range(4):
                out_ref[:, 128 * j:128 * j + 128] = v[j]
            out_ref[:, 512:576] = tail[:, 0:64]

        @pl.when(x % 2 == 1)
        def _():
            r = [pltpu.roll(w, 64, 1) for w in v]
            low = lax.broadcasted_iota(jnp.int32, (72, 128), 1) < 64
            out_ref[:, 0:128] = jnp.where(low, tail, r[0])
            for j in range(1, 4):
                out_ref[:, 128 * j:128 * j + 128] = jnp.where(low, r[j - 1], r[j])
            out_ref[:, 512:576] = r[3][:, 0:64]

    def valid(i):
        return (i >= 0) & (i < STEPS)

    def step(s, _):
        @pl.when(valid(s))
        def _():
            product(s)

        @pl.when(valid(s - 1))
        def _():
            relay(s - 1)

        @pl.when(s == 2)
        def _():
            send_b(twin_row, y_rows[0], 0).wait_recv()
            for cp in relays_b:
                cp.start()

        @pl.when(valid(s - 2))
        def _():
            gather(s - 2)

        i = s - LAG - z
        d = order(i)

        @pl.when(valid(i) & (d >= z))
        def _():
            @pl.when(z > 0)
            def _():
                z_copy(True, i).wait_recv()
                pu[i, x] += z_l[i]

            @pl.when(d > z)
            def _():
                z_copy(True, i).start()

        k = s - LAG - (7 - z)
        e = order(k)

        @pl.when(valid(k) & (e <= z))
        def _():
            @pl.when(z < 7)
            def _():
                z_copy(False, k).wait_recv()
                pu[k, x] += z_r[k]

            @pl.when(e < z)
            def _():
                z_copy(False, k).start()

        return 0

    lax.fori_loop(0, STEPS + LAG + 4, step, 0)

    def find(i, _):
        @pl.when(order(i) == z)
        def _():
            write_out(i)

        return 0

    lax.fori_loop(0, STEPS, find, 0)

    def drain(i, _):
        for kind in range(6):
            x_copy(kind, i).wait_send()

        @pl.when(order(i) != z)
        def _():
            z_copy(True, i).wait_send()

        return 0

    lax.fori_loop(0, STEPS, drain, 0)
    swap_b.wait_send()
    for cp in swap_a:
        cp.wait_send()
    for cp in sends_b + relays_b:
        cp.wait_send()


def per_device(amplitudes, cycle_ints):
    f32 = jnp.float32
    out = pl.pallas_call(
        kernel,
        out_shape=jax.ShapeDtypeStruct((72, 576), f32),
        in_specs=[pl.BlockSpec(memory_space=pl.ANY)] * 2,
        out_specs=pl.BlockSpec(memory_space=pltpu.VMEM),
        scratch_shapes=[
            pltpu.VMEM((288, 2304), f32),
            pltpu.VMEM((288, 2304), f32),
            pltpu.VMEM((576, 2304), jnp.bfloat16),
            pltpu.VMEM((576, 2304), jnp.bfloat16),
            pltpu.VMEM((144, 288), f32),
            pltpu.VMEM((72, 288), f32),
            pltpu.VMEM((8, 72, 640), f32),
            pltpu.VMEM((STEPS, NX, UNIT, 128), f32),
            pltpu.VMEM((STEPS, TOP, 128), f32),
            pltpu.VMEM((STEPS, BOT, 128), f32),
            pltpu.VMEM((STEPS, UNIT, 128), f32),
            pltpu.VMEM((STEPS, UNIT, 128), f32),
            pltpu.VMEM((STEPS, UNIT, 128), f32),
            pltpu.VMEM((STEPS, UNIT, 128), f32),
            pltpu.SemaphoreType.DMA((3,)),
            pltpu.SemaphoreType.DMA((3,)),
            pltpu.SemaphoreType.DMA((3,)),
            pltpu.SemaphoreType.DMA((7,)),
            pltpu.SemaphoreType.DMA((8,)),
            pltpu.SemaphoreType.DMA((6, STEPS)),
            pltpu.SemaphoreType.DMA((6, STEPS)),
            pltpu.SemaphoreType.DMA((1, STEPS)),
            pltpu.SemaphoreType.DMA((2, STEPS)),
        ],
        compiler_params=pltpu.CompilerParams(
            collective_id=0, has_side_effects=True, vmem_limit_bytes=48 * 2**20
        ),
        cost_estimate=pl.CostEstimate(
            flops=6 * 2304 * 576 * 576, bytes_accessed=3 * 2**20, transcendentals=0
        ),
        name="cycle_term",
    )(amplitudes.T, cycle_ints.T)
    return out.T


def solution(mesh):
    return jax.shard_map(
        per_device,
        mesh=mesh,
        in_specs=(P("row", ("col", "rep")), P(("col", "rep"), "row")),
        out_specs=P(("row", "rep"), "col"),
        check_vma=False,
    )
```

```python
import functools

import jax
import jax.numpy as jnp
from jax import lax
from jax.experimental import pallas as pl
from jax.experimental.pallas import tpu as pltpu
from jax.sharding import PartitionSpec as P

MESH = pl.DeviceIdType.MESH
STEPS = 8
NX = 4
TOP = 160
UNIT = 328
BOT = UNIT - TOP
PARTS = ((0, 88), (88, 80), (168, 80), (248, 80))
LAGS = (2, 1)
BASES = (5, 13)
TURNS = 12
ISSUED = (2, 3, 4, 4, 5, 7, 8)


def split(value):
    high = value.astype(jnp.bfloat16)
    return high, (value - high.astype(jnp.float32)).astype(jnp.bfloat16)


def kernel(
    at_ref, bt_ref, out_ref,
    a_own, a_oth, ah, al, b_own, b_oth, bq, pu, opp_l, opp_r, in_l, in_r, z_in,
    loc_sem, core_s, core_r, b_s, b_r, x_s, x_r, z_s, z_rs, z_ready, h_ready,
):
    row, col, x = lax.axis_index("row"), lax.axis_index("col"), lax.axis_index("rep")
    y, h = row // 2, row % 2
    z, c = col // 2, col % 2
    other = {"col": col + 1 - 2 * c}
    right, left, opp = (x + 1) % NX, (x + 3) % NX, (x + 2) % NX
    to_right, to_left = {"rep": right}, {"rep": left}
    twin_row = row + 1 - 2 * h
    y_rows = [(row + 2) % 8, (row + 6) % 8, (row + 4) % 8]
    spans = [pl.ds(pl.multiple_of(1152 * p, 128), 1152) for p in (1 - x // 2, x // 2)]

    load_b = pltpu.make_async_copy(bt_ref, b_own, loc_sem.at[2])
    load_b.start()
    load_a = [
        pltpu.make_async_copy(at_ref.at[:, span], a_own.at[:, span], loc_sem.at[n])
        for n, span in enumerate(spans)
    ]
    for cp in load_a:
        cp.start()

    barrier = pltpu.get_barrier_semaphore()

    def greet(device, sem=barrier):
        pl.semaphore_signal(sem, inc=1, device_id=device, device_id_type=MESH)

    greet(other)
    greet(to_right)
    greet(to_left)
    for r in y_rows:
        greet({"row": r})

    @pl.when(z < 7)
    def _():
        greet({"col": col + 2})

    @pl.when(h == 0)
    def _():
        greet({"row": twin_row})

    pl.semaphore_wait(barrier, 6 + jnp.minimum(z, 1) + h)

    @pl.when(z > 0)
    def _():
        greet({"col": col - 2}, z_ready)

    @pl.when(h == 1)
    def _():
        greet({"row": twin_row}, h_ready)

    load_b.wait()
    swap_b = pltpu.make_async_remote_copy(
        b_own.at[pl.ds((1 - c) * 72, 72)], b_oth, core_s.at[0], core_r.at[0],
        device_id=other, device_id_type=MESH,
    )
    swap_b.start()
    swap_a = []
    for n, span in enumerate(spans):
        load_a[n].wait()
        cp = pltpu.make_async_remote_copy(
            a_own.at[:, span], a_oth.at[:, span],
            core_s.at[1 + n], core_r.at[1 + n], device_id=other, device_id_type=MESH,
        )
        cp.start()
        swap_a.append(cp)
    swap_b.wait_recv()
    mine = jnp.concatenate([b_own[pl.ds(c * 72, 72), :], b_oth[...]], axis=1)
    for j in range(4):
        bq[row, 72 * j:72 * j + 72, :] = mine[:, 128 * j:128 * j + 128]
    bq[row, 288:328, :] = jnp.concatenate([mine[0:40, 512:576], mine[32:72, 512:576]], axis=1)

    def send_b(slot, target, sem):
        return pltpu.make_async_remote_copy(
            bq.at[slot], bq.at[slot], b_s.at[sem], b_r.at[slot],
            device_id={"row": target}, device_id_type=MESH,
        )

    to_twin = send_b(row, twin_row, 0)

    @pl.when(h == 1)
    def _():
        to_twin.start()

    sends_b = [send_b(row, r, 1 + n) for n, r in enumerate(y_rows)]
    for cp in sends_b:
        cp.start()
    relays_b = [send_b(twin_row, r, 4 + n) for n, r in enumerate(y_rows)]

    def convert(source, base, n):
        span = spans[n]

        def some(i, _):
            rows = pl.ds(pl.multiple_of(i * 16, 16), 16)
            into = pl.ds(pl.multiple_of(base + i * 16, 16), 16)
            high, low = split(source[rows, span])
            ah[into, span] = high
            al[into, span] = low
            return 0

        lax.fori_loop(0, 18, some, 0, unroll=6)

    def by_distance(parity, first):
        blocks = [2 * a + parity for a in range(4)]
        keys = [
            2 * jnp.abs(d - z) + jnp.where(d > z, 1, 0) + jnp.where(d == first, 100, 0) for d in blocks
        ]
        ranks = [sum(jnp.where(other > key, 1, 0) for other in keys) for key in keys]
        return [sum(jnp.where(r == j, d, 0) for r, d in zip(ranks, blocks)) for j in range(4)]

    listed = by_distance(h, row) + by_distance(1 - h, twin_row)

    def order(i):
        d = listed[0]
        for n in range(1, STEPS):
            d = jnp.where(i == n, listed[n], d)
        return d

    lanes = lax.broadcasted_iota(jnp.int32, (40, 128), 1)

    def x_copy(kind, i):
        top, bot = pl.ds(0, TOP), pl.ds(TOP, BOT)
        src, dst, device = (
            (pu.at[i, opp, top], opp_l.at[i], to_right),
            (pu.at[i, opp, bot], opp_r.at[i], to_left),
            (pu.at[i, right, bot], in_l.at[i, bot], to_right),
            (pu.at[i, left, top], in_r.at[i, top], to_left),
            (pu.at[i, right, top], in_l.at[i, top], to_right),
            (pu.at[i, left, bot], in_r.at[i, bot], to_left),
        )[kind]
        return pltpu.make_async_remote_copy(
            src, dst, x_s.at[kind, i], x_r.at[kind, i], device_id=device, device_id_type=MESH
        )

    def z_copy(down, d, piece):
        part = pl.ds(*PARTS[piece])
        return pltpu.make_async_remote_copy(
            pu.at[d, x, part], z_in.at[down, d, part], z_s.at[piece, d], z_rs.at[piece, down, d],
            device_id={"col": col + 2 - 4 * down}, device_id_type=MESH,
        )

    def z_add(down, d, piece):
        part = slice(PARTS[piece][0], sum(PARTS[piece]))
        z_copy(down, d, piece).wait_recv()
        pu[d, x, part, :] += z_in[down, d, part, :]

    def half_product(i, b_parts, n):
        bh, bl = b_parts
        p = x // 2 if n else 1 - x // 2
        span = spans[n]
        high = ah[:, span]
        v = jnp.dot(bh, high, preferred_element_type=jnp.float32)
        v += jnp.dot(bl, high, preferred_element_type=jnp.float32)
        v += jnp.dot(bh, al[:, span], preferred_element_type=jnp.float32)
        for j in range(4):
            pu[i, 2 * p, 72 * j:72 * j + 72, :] = v[:, 128 * j:128 * j + 128]
            pu[i, 2 * p + 1, 72 * j:72 * j + 72, :] = v[:, 640 + 128 * j:768 + 128 * j]
        up, down = v[0:40, 512:640], v[32:72, 512:640]
        pu[i, 2 * p, 288:328, :] = jnp.where(lanes < 64, up, pltpu.roll(down, 64, 1))
        pu[i, 2 * p + 1, 288:328, :] = jnp.where(lanes < 64, pltpu.roll(up, 64, 1), down)
        x_copy(2 * n, i).start()
        x_copy(2 * n + 1, i).start()

    def b_of(d):
        tail = bq[d, 288:328, :]
        tail = jnp.concatenate([tail, pltpu.roll(tail, 64, 1)[8:40]], axis=0)
        tiles = [bq[d, 72 * j:72 * j + 72, :] for j in range(4)]
        return split(jnp.concatenate(tiles + [tail[:, 0:64]], axis=1))

    def product(d):
        @pl.when((d != row) & (d != twin_row))
        def _():
            send_b(d, twin_row, 0).wait_recv()

        parts = b_of(d)
        half_product(d, parts, 0)
        half_product(d, parts, 1)

    def relay(i):
        x_copy(0, i).wait_recv()
        pu[i, right, 0:TOP, :] += opp_l[i]
        x_copy(4, i).start()
        x_copy(1, i).wait_recv()
        pu[i, left, TOP:UNIT, :] += opp_r[i]
        x_copy(5, i).start()

    def gather(i):
        for kind in (2, 4, 3, 5):
            x_copy(kind, i).wait_recv()
        pu[i, x] += in_l[i] + in_r[i]

    def write_out(i):
        v = [pu[i, x, 72 * j:72 * j + 72, :] for j in range(4)]
        tail = pu[i, x, 288:328, :]
        tail = jnp.concatenate([tail, pltpu.roll(tail, 64, 1)[8:40]], axis=0)

        @pl.when(x % 2 == 0)
        def _():
            for j in range(4):
                out_ref[:, 128 * j:128 * j + 128] = v[j]
            out_ref[:, 512:576] = tail[:, 0:64]

        @pl.when(x % 2 == 1)
        def _():
            r = [pltpu.roll(w, 64, 1) for w in v]
            low = lax.broadcasted_iota(jnp.int32, (72, 128), 1) < 64
            out_ref[:, 0:128] = jnp.where(low, tail, r[0])
            for j in range(1, 4):
                out_ref[:, 128 * j:128 * j + 128] = jnp.where(low, r[j - 1], r[j])
            out_ref[:, 512:576] = r[3][:, 0:64]

    def z_tasks(slot):
        def one(i, _):
            d = order(i)
            down = jnp.where(d < z, 1, 0)
            hop = jnp.where(d < z, 7 - z, z)
            late = jnp.where(i < 4, BASES[0] + LAGS[0] * hop, BASES[1] + LAGS[1] * hop)
            late += jnp.where(i % 4 > 0, 2, 0)

            @pl.when((d != z) & (jnp.maximum(2 * i + 5, late) == slot))
            def _():
                for piece in range(len(PARTS)):
                    @pl.when(hop > 0)
                    def _():
                        z_add(down, d, piece)

                    z_copy(down, d, piece).start()

            return 0

        lax.fori_loop(0, STEPS, one, 0)

    def valid(i):
        return (i >= 0) & (i < STEPS)

    convert(a_own, 0, 0)
    convert(a_own, 0, 1)
    first_b = b_of(row)
    for n in range(2):
        swap_a[n].wait_recv()
        convert(a_oth, 288, n)
        half_product(row, first_b, n)

    @pl.when(z < 7)
    def _():
        pl.semaphore_wait(z_ready, 1)

    def issued(s):
        count = 1
        for turn, n in enumerate(ISSUED):
            count = jnp.where(s >= turn, n, count)
        return count

    def step(s, _):
        @pl.when(valid(s - 1))
        def _():
            relay(order(s - 1))

        @pl.when((s == 1) & (h == 0))
        def _():
            pl.semaphore_wait(h_ready, 1)
            to_twin.start()

        @pl.when(s == 4 - h)
        def _():
            send_b(twin_row, y_rows[0], 0).wait_recv()
            for cp in relays_b:
                cp.start()

        def some(i, _):
            product(order(i))
            return 0

        lax.fori_loop(issued(s - 1), issued(s), some, 0)

        z_tasks(2 * s)

        @pl.when(valid(s - 2))
        def _():
            gather(order(s - 2))

        z_tasks(2 * s + 1)
        return 0

    lax.fori_loop(0, TURNS, step, 0)

    for piece in range(len(PARTS)):
        @pl.when(z > 0)
        def _():
            z_add(0, z, piece)

        @pl.when(z < 7)
        def _():
            z_add(1, z, piece)

    write_out(z)

    def drain(i, _):
        for kind in range(6):
            x_copy(kind, i).wait_send()

        @pl.when(i != z)
        def _():
            for piece in range(len(PARTS)):
                z_copy(0, i, piece).wait_send()

        return 0

    lax.fori_loop(0, STEPS, drain, 0)
    swap_b.wait_send()
    for cp in swap_a:
        cp.wait_send()
    to_twin.wait_send()
    for cp in sends_b + relays_b:
        cp.wait_send()


def per_device(amplitudes, cycle_ints):
    f32 = jnp.float32
    out = pl.pallas_call(
        kernel,
        out_shape=jax.ShapeDtypeStruct((72, 576), f32),
        in_specs=[pl.BlockSpec(memory_space=pl.ANY)] * 2,
        out_specs=pl.BlockSpec(memory_space=pltpu.VMEM),
        scratch_shapes=[
            pltpu.VMEM((288, 2304), f32),
            pltpu.VMEM((288, 2304), f32),
            pltpu.VMEM((576, 2304), jnp.bfloat16),
            pltpu.VMEM((576, 2304), jnp.bfloat16),
            pltpu.VMEM((144, 288), f32),
            pltpu.VMEM((72, 288), f32),
            pltpu.VMEM((8, UNIT, 128), f32),
            pltpu.VMEM((STEPS, NX, UNIT, 128), f32),
            pltpu.VMEM((STEPS, TOP, 128), f32),
            pltpu.VMEM((STEPS, BOT, 128), f32),
            pltpu.VMEM((STEPS, UNIT, 128), f32),
            pltpu.VMEM((STEPS, UNIT, 128), f32),
            pltpu.VMEM((2, STEPS, UNIT, 128), f32),
            pltpu.SemaphoreType.DMA((3,)),
            pltpu.SemaphoreType.DMA((3,)),
            pltpu.SemaphoreType.DMA((3,)),
            pltpu.SemaphoreType.DMA((7,)),
            pltpu.SemaphoreType.DMA((8,)),
            pltpu.SemaphoreType.DMA((6, STEPS)),
            pltpu.SemaphoreType.DMA((6, STEPS)),
            pltpu.SemaphoreType.DMA((len(PARTS), STEPS)),
            pltpu.SemaphoreType.DMA((len(PARTS), 2, STEPS)),
            pltpu.SemaphoreType.REGULAR,
            pltpu.SemaphoreType.REGULAR,
        ],
        compiler_params=pltpu.CompilerParams(
            collective_id=0, has_side_effects=True, vmem_limit_bytes=60 * 2**20
        ),
        cost_estimate=pl.CostEstimate(
            flops=6 * 2304 * 576 * 576, bytes_accessed=3 * 2**20, transcendentals=0
        ),
        name="cycle_term",
    )(amplitudes.T, cycle_ints.T)
    return out.T


def solution(mesh):
    return jax.shard_map(
        per_device,
        mesh=mesh,
        in_specs=(P("row", ("col", "rep")), P(("col", "rep"), "row")),
        out_specs=P(("row", "rep"), "col"),
        check_vma=False,
    )
```

```python
import functools

import jax
import jax.numpy as jnp
from jax import lax
from jax.experimental import pallas as pl
from jax.experimental.pallas import tpu as pltpu
from jax.sharding import PartitionSpec as P

MESH = pl.DeviceIdType.MESH
STEPS = 8
NX = 4
TOP = 160
UNIT = 328
BOT = UNIT - TOP
PARTS = ((0, 88), (88, 80), (168, 80), (248, 80))
LAGS = (2, 1)
BASES = (5, 13)
TURNS = 11
ISSUED = (2, 3, 4, 4, 5, 7, 8)


def split(value):
    high = value.astype(jnp.bfloat16)
    return high, (value - high.astype(jnp.float32)).astype(jnp.bfloat16)


def kernel(
    at_ref, bt_ref, out_ref,
    a_own, a_oth, ah, al, b_own, b_oth, bq, pu, opp_l, opp_r, in_l, in_r, z_in,
    loc_sem, core_s, core_r, b_s, b_r, x_s, x_r, z_s, z_rs, z_ready, h_ready,
):
    row, col, x = lax.axis_index("row"), lax.axis_index("col"), lax.axis_index("rep")
    y, h = row // 2, row % 2
    z, c = col // 2, col % 2
    other = {"col": col + 1 - 2 * c}
    right, left, opp = (x + 1) % NX, (x + 3) % NX, (x + 2) % NX
    to_right, to_left = {"rep": right}, {"rep": left}
    twin_row = row + 1 - 2 * h
    y_rows = [(row + 2) % 8, (row + 6) % 8, (row + 4) % 8]
    spans = [pl.ds(pl.multiple_of(1152 * p, 128), 1152) for p in (1 - x // 2, x // 2)]

    load_b = pltpu.make_async_copy(bt_ref, b_own, loc_sem.at[2])
    load_b.start()
    load_a = [
        pltpu.make_async_copy(at_ref.at[:, span], a_own.at[:, span], loc_sem.at[n])
        for n, span in enumerate(spans)
    ]
    for cp in load_a:
        cp.start()

    barrier = pltpu.get_barrier_semaphore()

    def greet(device, sem=barrier):
        pl.semaphore_signal(sem, inc=1, device_id=device, device_id_type=MESH)

    greet(other)
    greet(to_right)
    greet(to_left)
    for r in y_rows:
        greet({"row": r})

    @pl.when(z < 7)
    def _():
        greet({"col": col + 2})

    @pl.when(h == 0)
    def _():
        greet({"row": twin_row})

    pl.semaphore_wait(barrier, 6 + jnp.minimum(z, 1) + h)

    @pl.when(z > 0)
    def _():
        greet({"col": col - 2}, z_ready)

    @pl.when(h == 1)
    def _():
        greet({"row": twin_row}, h_ready)

    load_b.wait()
    swap_b = pltpu.make_async_remote_copy(
        b_own.at[pl.ds((1 - c) * 72, 72)], b_oth, core_s.at[0], core_r.at[0],
        device_id=other, device_id_type=MESH,
    )
    swap_b.start()
    swap_a = []
    for n, span in enumerate(spans):
        load_a[n].wait()
        cp = pltpu.make_async_remote_copy(
            a_own.at[:, span], a_oth.at[:, span],
            core_s.at[1 + n], core_r.at[1 + n], device_id=other, device_id_type=MESH,
        )
        cp.start()
        swap_a.append(cp)
    swap_b.wait_recv()
    mine = jnp.concatenate([b_own[pl.ds(c * 72, 72), :], b_oth[...]], axis=1)
    for j in range(4):
        bq[row, 72 * j:72 * j + 72, :] = mine[:, 128 * j:128 * j + 128]
    bq[row, 288:328, :] = jnp.concatenate([mine[0:40, 512:576], mine[32:72, 512:576]], axis=1)

    def send_b(slot, target, sem):
        return pltpu.make_async_remote_copy(
            bq.at[slot], bq.at[slot], b_s.at[sem], b_r.at[slot],
            device_id={"row": target}, device_id_type=MESH,
        )

    to_twin = send_b(row, twin_row, 0)

    @pl.when(h == 1)
    def _():
        to_twin.start()

    sends_b = [send_b(row, r, 1 + n) for n, r in enumerate(y_rows)]
    for cp in sends_b:
        cp.start()
    relays_b = [send_b(twin_row, r, 4 + n) for n, r in enumerate(y_rows)]

    def convert(source, base, n):
        span = spans[n]

        def some(i, _):
            rows = pl.ds(pl.multiple_of(i * 16, 16), 16)
            into = pl.ds(pl.multiple_of(base + i * 16, 16), 16)
            high, low = split(source[rows, span])
            ah[into, span] = high
            al[into, span] = low
            return 0

        lax.fori_loop(0, 18, some, 0, unroll=6)

    def by_distance(parity, first):
        blocks = [2 * a + parity for a in range(4)]
        keys = [
            2 * jnp.abs(d - z) + jnp.where(d > z, 1, 0) + jnp.where(d == first, 100, 0) for d in blocks
        ]
        ranks = [sum(jnp.where(other > key, 1, 0) for other in keys) for key in keys]
        return [sum(jnp.where(r == j, d, 0) for r, d in zip(ranks, blocks)) for j in range(4)]

    listed = by_distance(h, row) + by_distance(1 - h, twin_row)

    def order(i):
        d = listed[0]
        for n in range(1, STEPS):
            d = jnp.where(i == n, listed[n], d)
        return d

    lanes = lax.broadcasted_iota(jnp.int32, (40, 128), 1)

    def x_copy(kind, i):
        top, bot = pl.ds(0, TOP), pl.ds(TOP, BOT)
        src, dst, device = (
            (pu.at[i, opp, top], opp_l.at[i], to_right),
            (pu.at[i, opp, bot], opp_r.at[i], to_left),
            (pu.at[i, right, bot], in_l.at[i, bot], to_right),
            (pu.at[i, left, top], in_r.at[i, top], to_left),
            (pu.at[i, right, top], in_l.at[i, top], to_right),
            (pu.at[i, left, bot], in_r.at[i, bot], to_left),
        )[kind]
        return pltpu.make_async_remote_copy(
            src, dst, x_s.at[kind, i], x_r.at[kind, i], device_id=device, device_id_type=MESH
        )

    def z_copy(down, d, piece):
        part = pl.ds(*PARTS[piece])
        return pltpu.make_async_remote_copy(
            pu.at[d, x, part], z_in.at[down, d, part], z_s.at[piece, d], z_rs.at[piece, down, d],
            device_id={"col": col + 2 - 4 * down}, device_id_type=MESH,
        )

    def z_add(down, d, piece):
        part = slice(PARTS[piece][0], sum(PARTS[piece]))
        z_copy(down, d, piece).wait_recv()
        pu[d, x, part, :] += z_in[down, d, part, :]

    def half_product(i, b_parts, n):
        bh, bl = b_parts
        p = x // 2 if n else 1 - x // 2
        span = spans[n]
        high = ah[:, span]
        v = jnp.dot(bh, high, preferred_element_type=jnp.float32)
        v += jnp.dot(bl, high, preferred_element_type=jnp.float32)
        v += jnp.dot(bh, al[:, span], preferred_element_type=jnp.float32)
        for j in range(4):
            pu[i, 2 * p, 72 * j:72 * j + 72, :] = v[:, 128 * j:128 * j + 128]
            pu[i, 2 * p + 1, 72 * j:72 * j + 72, :] = v[:, 640 + 128 * j:768 + 128 * j]
        up, down = v[0:40, 512:640], v[32:72, 512:640]
        pu[i, 2 * p, 288:328, :] = jnp.where(lanes < 64, up, pltpu.roll(down, 64, 1))
        pu[i, 2 * p + 1, 288:328, :] = jnp.where(lanes < 64, pltpu.roll(up, 64, 1), down)
        x_copy(2 * n, i).start()
        x_copy(2 * n + 1, i).start()

    def b_of(d):
        tail = bq[d, 288:328, :]
        tail = jnp.concatenate([tail, pltpu.roll(tail, 64, 1)[8:40]], axis=0)
        tiles = [bq[d, 72 * j:72 * j + 72, :] for j in range(4)]
        return split(jnp.concatenate(tiles + [tail[:, 0:64]], axis=1))

    def product(d):
        @pl.when((d != row) & (d != twin_row))
        def _():
            send_b(d, twin_row, 0).wait_recv()

        parts = b_of(d)
        half_product(d, parts, 0)
        half_product(d, parts, 1)

    def relay(i):
        x_copy(0, i).wait_recv()
        pu[i, right, 0:TOP, :] += opp_l[i]
        x_copy(4, i).start()
        x_copy(1, i).wait_recv()
        pu[i, left, TOP:UNIT, :] += opp_r[i]
        x_copy(5, i).start()

    def gather(i):
        for kind in (2, 4, 3, 5):
            x_copy(kind, i).wait_recv()
        pu[i, x] += in_l[i] + in_r[i]

    def write_out(i):
        v = [pu[i, x, 72 * j:72 * j + 72, :] for j in range(4)]
        tail = pu[i, x, 288:328, :]
        tail = jnp.concatenate([tail, pltpu.roll(tail, 64, 1)[8:40]], axis=0)

        @pl.when(x % 2 == 0)
        def _():
            for j in range(4):
                out_ref[:, 128 * j:128 * j + 128] = v[j]
            out_ref[:, 512:576] = tail[:, 0:64]

        @pl.when(x % 2 == 1)
        def _():
            r = [pltpu.roll(w, 64, 1) for w in v]
            low = lax.broadcasted_iota(jnp.int32, (72, 128), 1) < 64
            out_ref[:, 0:128] = jnp.where(low, tail, r[0])
            for j in range(1, 4):
                out_ref[:, 128 * j:128 * j + 128] = jnp.where(low, r[j - 1], r[j])
            out_ref[:, 512:576] = r[3][:, 0:64]

    def due_of(i):
        d, first = listed[i], (row if i < 4 else twin_row)
        g = i // 4
        lower = jnp.where(d < z, 1, 0)
        ahead = jnp.where(d < z, d // 2, 3 - d // 2)
        ahead += 1 - jnp.where(d < z, jnp.where(first < d, 1, 0), jnp.where(first > d, 1, 0))
        start = BASES[g] + jnp.where(d == first, 0, 2 * ahead)
        hop = jnp.where(d < z, 7 - z, z)
        due = jnp.maximum(2 * i + 5, start + LAGS[g] * hop)
        return lower, hop, jnp.where(d == z, -1, due)

    dues = [due_of(i) for i in range(STEPS)]

    def z_tasks(slot):
        for d, (down, hop, due) in zip(listed, dues):
            @pl.when(due == slot)
            def _():
                for piece in range(len(PARTS)):
                    @pl.when(hop > 0)
                    def _():
                        z_add(down, d, piece)

                    z_copy(down, d, piece).start()

    def valid(i):
        return (i >= 0) & (i < STEPS)

    convert(a_own, 0, 0)
    convert(a_own, 0, 1)
    first_b = b_of(row)
    for n in range(2):
        swap_a[n].wait_recv()
        convert(a_oth, 288, n)
        half_product(row, first_b, n)

    @pl.when(z < 7)
    def _():
        pl.semaphore_wait(z_ready, 1)

    def issued(s):
        count = 1
        for turn, n in enumerate(ISSUED):
            count = jnp.where(s >= turn, n, count)
        return count

    def step(s, _):
        @pl.when(valid(s - 1))
        def _():
            relay(order(s - 1))

        @pl.when((s == 1) & (h == 0))
        def _():
            pl.semaphore_wait(h_ready, 1)
            to_twin.start()

        @pl.when(s == 3 + h)
        def _():
            send_b(twin_row, y_rows[0], 0).wait_recv()
            for cp in relays_b:
                cp.start()

        def some(i, _):
            product(order(i))
            return 0

        lax.fori_loop(issued(s - 1), issued(s), some, 0)

        z_tasks(2 * s)

        @pl.when(valid(s - 2))
        def _():
            gather(order(s - 2))

        z_tasks(2 * s + 1)
        return 0

    lax.fori_loop(0, TURNS, step, 0)

    def drain_x(i, _):
        for kind in range(6):
            x_copy(kind, i).wait_send()

        return 0

    lax.fori_loop(0, STEPS, drain_x, 0)
    swap_b.wait_send()
    for cp in swap_a:
        cp.wait_send()
    to_twin.wait_send()
    for cp in sends_b + relays_b:
        cp.wait_send()

    for piece in range(len(PARTS)):
        @pl.when(z > 0)
        def _():
            z_add(0, z, piece)

        @pl.when(z < 7)
        def _():
            z_add(1, z, piece)

    write_out(z)

    def drain_z(i, _):
        @pl.when(i != z)
        def _():
            for piece in range(len(PARTS)):
                z_copy(0, i, piece).wait_send()

        return 0

    lax.fori_loop(0, STEPS, drain_z, 0)


def per_device(amplitudes, cycle_ints):
    f32 = jnp.float32
    out = pl.pallas_call(
        kernel,
        out_shape=jax.ShapeDtypeStruct((72, 576), f32),
        in_specs=[pl.BlockSpec(memory_space=pl.ANY)] * 2,
        out_specs=pl.BlockSpec(memory_space=pltpu.VMEM),
        scratch_shapes=[
            pltpu.VMEM((288, 2304), f32),
            pltpu.VMEM((288, 2304), f32),
            pltpu.VMEM((576, 2304), jnp.bfloat16),
            pltpu.VMEM((576, 2304), jnp.bfloat16),
            pltpu.VMEM((144, 288), f32),
            pltpu.VMEM((72, 288), f32),
            pltpu.VMEM((8, UNIT, 128), f32),
            pltpu.VMEM((STEPS, NX, UNIT, 128), f32),
            pltpu.VMEM((STEPS, TOP, 128), f32),
            pltpu.VMEM((STEPS, BOT, 128), f32),
            pltpu.VMEM((STEPS, UNIT, 128), f32),
            pltpu.VMEM((STEPS, UNIT, 128), f32),
            pltpu.VMEM((2, STEPS, UNIT, 128), f32),
            pltpu.SemaphoreType.DMA((3,)),
            pltpu.SemaphoreType.DMA((3,)),
            pltpu.SemaphoreType.DMA((3,)),
            pltpu.SemaphoreType.DMA((7,)),
            pltpu.SemaphoreType.DMA((8,)),
            pltpu.SemaphoreType.DMA((6, STEPS)),
            pltpu.SemaphoreType.DMA((6, STEPS)),
            pltpu.SemaphoreType.DMA((len(PARTS), STEPS)),
            pltpu.SemaphoreType.DMA((len(PARTS), 2, STEPS)),
            pltpu.SemaphoreType.REGULAR,
            pltpu.SemaphoreType.REGULAR,
        ],
        compiler_params=pltpu.CompilerParams(
            collective_id=0, has_side_effects=True, vmem_limit_bytes=60 * 2**20
        ),
        cost_estimate=pl.CostEstimate(
            flops=6 * 2304 * 576 * 576, bytes_accessed=3 * 2**20, transcendentals=0
        ),
        name="cycle_term",
    )(amplitudes.T, cycle_ints.T)
    return out.T


def solution(mesh):
    return jax.shard_map(
        per_device,
        mesh=mesh,
        in_specs=(P("row", ("col", "rep")), P(("col", "rep"), "row")),
        out_specs=P(("row", "rep"), "col"),
        check_vma=False,
    )
```

```python
import functools

import jax
import jax.numpy as jnp
from jax import lax
from jax.experimental import pallas as pl
from jax.experimental.pallas import tpu as pltpu
from jax.sharding import PartitionSpec as P

MESH = pl.DeviceIdType.MESH
STEPS = 8
NX = 4
TOP = 160
UNIT = 328
BOT = UNIT - TOP
PARTS = tuple((40 * n, 40) for n in range(7)) + ((280, 48),)
LAGS = (2, 1)
BASES = (5, 13)
TURNS = 11
ISSUED = (2, 3, 4, 4, 5, 7, 8)


def split(value):
    high = value.astype(jnp.bfloat16)
    return high, (value - high.astype(jnp.float32)).astype(jnp.bfloat16)


def kernel(
    at_ref, bt_ref, out_ref,
    a_own, a_oth, ah, al, b_own, b_oth, bq, pu, opp_l, opp_r, in_l, in_r, z_in,
    loc_sem, core_s, core_r, b_s, b_r, x_s, x_r, z_s, z_rs, z_ready, h_ready,
):
    row, col, x = lax.axis_index("row"), lax.axis_index("col"), lax.axis_index("rep")
    y, h = row // 2, row % 2
    z, c = col // 2, col % 2
    other = {"col": col + 1 - 2 * c}
    right, left, opp = (x + 1) % NX, (x + 3) % NX, (x + 2) % NX
    to_right, to_left = {"rep": right}, {"rep": left}
    twin_row = row + 1 - 2 * h
    y_rows = [(row + 2) % 8, (row + 6) % 8, (row + 4) % 8]
    spans = [pl.ds(pl.multiple_of(1152 * p, 128), 1152) for p in (1 - x // 2, x // 2)]

    load_b = pltpu.make_async_copy(bt_ref, b_own, loc_sem.at[2])
    load_b.start()
    load_a = [
        pltpu.make_async_copy(at_ref.at[:, span], a_own.at[:, span], loc_sem.at[n])
        for n, span in enumerate(spans)
    ]
    for cp in load_a:
        cp.start()

    barrier = pltpu.get_barrier_semaphore()

    def greet(device, sem=barrier):
        pl.semaphore_signal(sem, inc=1, device_id=device, device_id_type=MESH)

    greet(other)
    greet(to_right)
    greet(to_left)
    for r in y_rows:
        greet({"row": r})

    @pl.when(z < 7)
    def _():
        greet({"col": col + 2})

    @pl.when(h == 0)
    def _():
        greet({"row": twin_row})

    pl.semaphore_wait(barrier, 6 + jnp.minimum(z, 1) + h)

    @pl.when(z > 0)
    def _():
        greet({"col": col - 2}, z_ready)

    @pl.when(h == 1)
    def _():
        greet({"row": twin_row}, h_ready)

    load_b.wait()
    swap_b = pltpu.make_async_remote_copy(
        b_own.at[pl.ds((1 - c) * 72, 72)], b_oth, core_s.at[0], core_r.at[0],
        device_id=other, device_id_type=MESH,
    )
    swap_b.start()
    swap_a = []
    for n, span in enumerate(spans):
        load_a[n].wait()
        cp = pltpu.make_async_remote_copy(
            a_own.at[:, span], a_oth.at[:, span],
            core_s.at[1 + n], core_r.at[1 + n], device_id=other, device_id_type=MESH,
        )
        cp.start()
        swap_a.append(cp)
    swap_b.wait_recv()
    mine = jnp.concatenate([b_own[pl.ds(c * 72, 72), :], b_oth[...]], axis=1)
    for j in range(4):
        bq[row, 72 * j:72 * j + 72, :] = mine[:, 128 * j:128 * j + 128]
    bq[row, 288:328, :] = jnp.concatenate([mine[0:40, 512:576], mine[32:72, 512:576]], axis=1)

    def send_b(slot, target, sem):
        return pltpu.make_async_remote_copy(
            bq.at[slot], bq.at[slot], b_s.at[sem], b_r.at[slot],
            device_id={"row": target}, device_id_type=MESH,
        )

    to_twin = send_b(row, twin_row, 0)

    @pl.when(h == 1)
    def _():
        to_twin.start()

    sends_b = [send_b(row, r, 1 + n) for n, r in enumerate(y_rows)]
    for cp in sends_b:
        cp.start()
    relays_b = [send_b(twin_row, r, 4 + n) for n, r in enumerate(y_rows)]

    def convert(source, base, n):
        span = spans[n]

        def some(i, _):
            rows = pl.ds(pl.multiple_of(i * 16, 16), 16)
            into = pl.ds(pl.multiple_of(base + i * 16, 16), 16)
            high, low = split(source[rows, span])
            ah[into, span] = high
            al[into, span] = low
            return 0

        lax.fori_loop(0, 18, some, 0, unroll=6)

    def by_distance(parity, first):
        blocks = [2 * a + parity for a in range(4)]
        keys = [
            2 * jnp.abs(d - z) + jnp.where(d > z, 1, 0) + jnp.where(d == first, 100, 0) for d in blocks
        ]
        ranks = [sum(jnp.where(other > key, 1, 0) for other in keys) for key in keys]
        return [sum(jnp.where(r == j, d, 0) for r, d in zip(ranks, blocks)) for j in range(4)]

    listed = by_distance(h, row) + by_distance(1 - h, twin_row)

    def order(i):
        d = listed[0]
        for n in range(1, STEPS):
            d = jnp.where(i == n, listed[n], d)
        return d

    lanes = lax.broadcasted_iota(jnp.int32, (40, 128), 1)

    def x_copy(kind, i):
        top, bot = pl.ds(0, TOP), pl.ds(TOP, BOT)
        src, dst, device = (
            (pu.at[i, opp, top], opp_l.at[i], to_right),
            (pu.at[i, opp, bot], opp_r.at[i], to_left),
            (pu.at[i, right, bot], in_l.at[i, bot], to_right),
            (pu.at[i, left, top], in_r.at[i, top], to_left),
            (pu.at[i, right, top], in_l.at[i, top], to_right),
            (pu.at[i, left, bot], in_r.at[i, bot], to_left),
        )[kind]
        return pltpu.make_async_remote_copy(
            src, dst, x_s.at[kind, i], x_r.at[kind, i], device_id=device, device_id_type=MESH
        )

    def z_copy(down, d, piece):
        part = pl.ds(*PARTS[piece])
        return pltpu.make_async_remote_copy(
            pu.at[d, x, part], z_in.at[down, d, part], z_s.at[piece, d], z_rs.at[piece, down, d],
            device_id={"col": col + 2 - 4 * down}, device_id_type=MESH,
        )

    def z_add(down, d, piece):
        part = slice(PARTS[piece][0], sum(PARTS[piece]))
        z_copy(down, d, piece).wait_recv()
        pu[d, x, part, :] += z_in[down, d, part, :]

    def half_product(i, b_parts, n):
        bh, bl = b_parts
        p = x // 2 if n else 1 - x // 2
        span = spans[n]
        high = ah[:, span]
        v = jnp.dot(bh, high, preferred_element_type=jnp.float32)
        v += jnp.dot(bl, high, preferred_element_type=jnp.float32)
        v += jnp.dot(bh, al[:, span], preferred_element_type=jnp.float32)
        for j in range(4):
            pu[i, 2 * p, 72 * j:72 * j + 72, :] = v[:, 128 * j:128 * j + 128]
            pu[i, 2 * p + 1, 72 * j:72 * j + 72, :] = v[:, 640 + 128 * j:768 + 128 * j]
        up, down = v[0:40, 512:640], v[32:72, 512:640]
        pu[i, 2 * p, 288:328, :] = jnp.where(lanes < 64, up, pltpu.roll(down, 64, 1))
        pu[i, 2 * p + 1, 288:328, :] = jnp.where(lanes < 64, pltpu.roll(up, 64, 1), down)
        x_copy(2 * n, i).start()
        x_copy(2 * n + 1, i).start()

    def b_of(d):
        tail = bq[d, 288:328, :]
        tail = jnp.concatenate([tail, pltpu.roll(tail, 64, 1)[8:40]], axis=0)
        tiles = [bq[d, 72 * j:72 * j + 72, :] for j in range(4)]
        return split(jnp.concatenate(tiles + [tail[:, 0:64]], axis=1))

    def product(d):
        @pl.when((d != row) & (d != twin_row))
        def _():
            send_b(d, twin_row, 0).wait_recv()

        parts = b_of(d)
        half_product(d, parts, 0)
        half_product(d, parts, 1)

    def relay(i):
        x_copy(0, i).wait_recv()
        pu[i, right, 0:TOP, :] += opp_l[i]
        x_copy(4, i).start()
        x_copy(1, i).wait_recv()
        pu[i, left, TOP:UNIT, :] += opp_r[i]
        x_copy(5, i).start()

    def gather(i):
        for kind in (2, 4, 3, 5):
            x_copy(kind, i).wait_recv()
        pu[i, x] += in_l[i] + in_r[i]

    def write_out(i):
        v = [pu[i, x, 72 * j:72 * j + 72, :] for j in range(4)]
        tail = pu[i, x, 288:328, :]
        tail = jnp.concatenate([tail, pltpu.roll(tail, 64, 1)[8:40]], axis=0)

        @pl.when(x % 2 == 0)
        def _():
            for j in range(4):
                out_ref[:, 128 * j:128 * j + 128] = v[j]
            out_ref[:, 512:576] = tail[:, 0:64]

        @pl.when(x % 2 == 1)
        def _():
            r = [pltpu.roll(w, 64, 1) for w in v]
            low = lax.broadcasted_iota(jnp.int32, (72, 128), 1) < 64
            out_ref[:, 0:128] = jnp.where(low, tail, r[0])
            for j in range(1, 4):
                out_ref[:, 128 * j:128 * j + 128] = jnp.where(low, r[j - 1], r[j])
            out_ref[:, 512:576] = r[3][:, 0:64]

    def due_of(i):
        d, first = listed[i], (row if i < 4 else twin_row)
        g = i // 4
        lower = jnp.where(d < z, 1, 0)
        ahead = jnp.where(d < z, d // 2, 3 - d // 2)
        ahead += 1 - jnp.where(d < z, jnp.where(first < d, 1, 0), jnp.where(first > d, 1, 0))
        start = BASES[g] + jnp.where(d == first, 0, 2 * ahead)
        hop = jnp.where(d < z, 7 - z, z)
        due = jnp.maximum(2 * i + 5, start + LAGS[g] * hop)
        return lower, hop, jnp.where(d == z, -1, due)

    dues = [due_of(i) for i in range(STEPS)]

    def z_tasks(slot):
        for d, (down, hop, due) in zip(listed, dues):
            @pl.when(due == slot)
            def _():
                for piece in range(len(PARTS)):
                    @pl.when(hop > 0)
                    def _():
                        z_add(down, d, piece)

                    z_copy(down, d, piece).start()

    def valid(i):
        return (i >= 0) & (i < STEPS)

    convert(a_own, 0, 0)
    convert(a_own, 0, 1)
    first_b = b_of(row)
    for n in range(2):
        swap_a[n].wait_recv()
        convert(a_oth, 288, n)
        half_product(row, first_b, n)

    @pl.when(z < 7)
    def _():
        pl.semaphore_wait(z_ready, 1)

    def issued(s):
        count = 1
        for turn, n in enumerate(ISSUED):
            count = jnp.where(s >= turn, n, count)
        return count

    def step(s, _):
        @pl.when(valid(s - 1))
        def _():
            relay(order(s - 1))

        @pl.when((s == 1) & (h == 0))
        def _():
            pl.semaphore_wait(h_ready, 1)
            to_twin.start()

        @pl.when(s == 3 + h)
        def _():
            send_b(twin_row, y_rows[0], 0).wait_recv()
            for cp in relays_b:
                cp.start()

        def some(i, _):
            product(order(i))
            return 0

        lax.fori_loop(issued(s - 1), issued(s), some, 0)

        z_tasks(2 * s)

        @pl.when(valid(s - 2))
        def _():
            gather(order(s - 2))

        z_tasks(2 * s + 1)
        return 0

    lax.fori_loop(0, TURNS, step, 0)

    def drain_x(i, _):
        for kind in range(6):
            x_copy(kind, i).wait_send()

        return 0

    lax.fori_loop(0, STEPS, drain_x, 0)
    swap_b.wait_send()
    for cp in swap_a:
        cp.wait_send()
    to_twin.wait_send()
    for cp in sends_b + relays_b:
        cp.wait_send()

    for piece in range(len(PARTS)):
        @pl.when(z > 0)
        def _():
            z_add(0, z, piece)

        @pl.when(z < 7)
        def _():
            z_add(1, z, piece)

    write_out(z)

    def drain_z(i, _):
        @pl.when(i != z)
        def _():
            for piece in range(len(PARTS)):
                z_copy(0, i, piece).wait_send()

        return 0

    lax.fori_loop(0, STEPS, drain_z, 0)


def per_device(amplitudes, cycle_ints):
    f32 = jnp.float32
    out = pl.pallas_call(
        kernel,
        out_shape=jax.ShapeDtypeStruct((72, 576), f32),
        in_specs=[pl.BlockSpec(memory_space=pl.ANY)] * 2,
        out_specs=pl.BlockSpec(memory_space=pltpu.VMEM),
        scratch_shapes=[
            pltpu.VMEM((288, 2304), f32),
            pltpu.VMEM((288, 2304), f32),
            pltpu.VMEM((576, 2304), jnp.bfloat16),
            pltpu.VMEM((576, 2304), jnp.bfloat16),
            pltpu.VMEM((144, 288), f32),
            pltpu.VMEM((72, 288), f32),
            pltpu.VMEM((8, UNIT, 128), f32),
            pltpu.VMEM((STEPS, NX, UNIT, 128), f32),
            pltpu.VMEM((STEPS, TOP, 128), f32),
            pltpu.VMEM((STEPS, BOT, 128), f32),
            pltpu.VMEM((STEPS, UNIT, 128), f32),
            pltpu.VMEM((STEPS, UNIT, 128), f32),
            pltpu.VMEM((2, STEPS, UNIT, 128), f32),
            pltpu.SemaphoreType.DMA((3,)),
            pltpu.SemaphoreType.DMA((3,)),
            pltpu.SemaphoreType.DMA((3,)),
            pltpu.SemaphoreType.DMA((7,)),
            pltpu.SemaphoreType.DMA((8,)),
            pltpu.SemaphoreType.DMA((6, STEPS)),
            pltpu.SemaphoreType.DMA((6, STEPS)),
            pltpu.SemaphoreType.DMA((len(PARTS), STEPS)),
            pltpu.SemaphoreType.DMA((len(PARTS), 2, STEPS)),
            pltpu.SemaphoreType.REGULAR,
            pltpu.SemaphoreType.REGULAR,
        ],
        compiler_params=pltpu.CompilerParams(
            collective_id=0, has_side_effects=True, vmem_limit_bytes=60 * 2**20
        ),
        cost_estimate=pl.CostEstimate(
            flops=6 * 2304 * 576 * 576, bytes_accessed=3 * 2**20, transcendentals=0
        ),
        name="cycle_term",
    )(amplitudes.T, cycle_ints.T)
    return out.T


def solution(mesh):
    return jax.shard_map(
        per_device,
        mesh=mesh,
        in_specs=(P("row", ("col", "rep")), P(("col", "rep"), "row")),
        out_specs=P(("row", "rep"), "col"),
        check_vma=False,
    )
```
